32 devices in a mesh: grp: 4 (over x, core), shard: 8 (over z, y).
Axes of the slice: x: 2, y: 2, z: 4, core: 2. Of those that a mesh axis runs over, the one named last changes fastest.
Arguments:
- activations: bfloat16 [1, 6144, 5120], P(None, ('grp', 'shard')), may hold values from -6 to 6
- out_grads: bfloat16 [1, 6144, 5120], P(None, ('grp', 'shard')), may hold values from -0.15234375 to 0.15234375
- error: float32 [4, 5120, 1, 5120], P('grp', 'shard'), may hold values from -6 to 6
- q_start: float32 [1, 32, 5120], replicated, may hold values from -6 to 6
Outputs:
- update: float32 [5120, 1, 5120], P('shard')
- error_next: float32 [4, 5120, 1, 5120], P('grp', 'shard')
- factor: float32 [1, 32, 5120], replicated
The draws below stay inside these ranges and needn't reach their ends.
All inputs are finite; a program needn't handle non-finite values.
Results may differ from the reference program's by a relative error of at most 0.0034.
Values may be sent and summed in bfloat16 or wider, within the bound.
A program may use at most 256 MiB of HBM per device.

```python
import jax
import jax.numpy as jnp
from jax import lax

DW = 5120
RANK = 32
MATS = 1
ITERS = 2
TOK_DEV = 192
GROUPS = 4
GROUP_TOK = 1536
TOKENS = 6144
N_SHARD = 8


def levels(own_key, extent, shards, low, largest):
    gain, own = 1.0, jax.random.fold_in(own_key, 6)
    for axis_at, blocks in shards:
        heights = jnp.exp(jax.random.uniform(jax.random.fold_in(own, axis_at), (blocks,), jnp.float32, low / len(shards), largest / len(shards)))
        gain = gain * jnp.repeat(heights, extent[axis_at] // blocks).reshape([-1 if axis == axis_at else 1 for axis in range(len(extent))])
    return gain


def bell_draw(key, extent, scale, limit, cuts=(), dtype=jnp.bfloat16):
    values = jax.random.normal(key, extent, jnp.float32) * scale
    if len(cuts) > 0:
        values = levels(key, extent, cuts, -0.22, 0.18) * values
    return jnp.clip(values, min=-limit, max=limit).astype(dtype)


def setup_inputs(seed: int = 0) -> dict:
    seeds = jax.random.split(jax.random.key(seed), 5)
    return {
        "activations": bell_draw(seeds[0], (MATS, TOKENS, DW), 1.0, 6.0, ((1, 32),)),
        "out_grads": bell_draw(seeds[1], (MATS, TOKENS, DW), (GROUP_TOK ** -0.5), 0.15234375, ((1, 32),)),
        "error": bell_draw(seeds[2], (GROUPS, DW, MATS, DW), 1.0, 6.0, ((0, 4), (1, 8)), jnp.float32),
        "q_start": bell_draw(seeds[3], (MATS, RANK, DW), 1.0, 6.0, (), jnp.float32),
    }


def group_gradient(pair):
    inputs, grads = pair

    def accumulate(running, piece):
        left_in, right_in = piece
        partial_sum = jnp.einsum('mta,mtc->amc', left_in.astype(jnp.float32), right_in.astype(jnp.float32))
        rounded = lax.optimization_barrier(partial_sum.astype(jnp.bfloat16)).astype(jnp.float32)
        return (running + rounded, None)
    start_sum = jnp.zeros((DW, MATS, DW), jnp.float32)
    running, unused = lax.scan(accumulate, start_sum, (inputs, grads))
    return running

def reference(activations, out_grads, error, q_start):
    shaped_in = activations.reshape(MATS, GROUPS, N_SHARD, TOK_DEV, DW).transpose(1, 2, 0, 3, 4)
    shaped_grad = out_grads.reshape(MATS, GROUPS, N_SHARD, TOK_DEV, DW).transpose(1, 2, 0, 3, 4)
    gradient = lax.map(group_gradient, (shaped_in, shaped_grad))
    momentum = gradient + error
    right = q_start
    high = lax.Precision.HIGHEST
    for step in range(ITERS):
        left = jnp.einsum('grmc,mkc->rmk', momentum, right, precision=high) / GROUPS
        gram = jnp.einsum('rmk,rml->mkl', left, left, precision=high)
        lower = jnp.linalg.cholesky(gram)
        basis = jax.vmap(lambda tri, rhs: jax.scipy.linalg.solve_triangular(tri, rhs, lower=True))(lower, left.transpose(1, 2, 0))
        right = jnp.einsum('mkr,grmc->mkc', basis, momentum, precision=high) / GROUPS
    update = jnp.einsum('mkr,mkc->rmc', basis, right, precision=high)
    return (update, momentum - update[None], right)
```

```python
import functools

import jax
import jax.numpy as jnp
from jax import lax
from jax.experimental import pallas as pl
from jax.experimental.pallas import tpu as pltpu
from jax.sharding import PartitionSpec as P

ITERS = 2
CHUNKS = 4
LANES = 128
F32 = jnp.float32
BF16 = jnp.bfloat16
NN = (((1,), (0,)), ((), ()))
NT = (((1,), (1,)), ((), ()))


def split(x):
    high = x.astype(BF16)
    return high, (x - high.astype(F32)).astype(BF16)


def dot2(x, y, dims):
    rows = x.shape[0]
    both = lax.dot_general(jnp.concatenate(split(x), axis=0), y, dims, preferred_element_type=F32)
    return both[:rows] + both[rows:]


def dot3(x, y_high, y_low, dims):
    return dot2(x, y_high, dims) + lax.dot_general(x.astype(BF16), y_low, dims, preferred_element_type=F32)


def inverse_lower(gram):
    n = gram.shape[0]
    row = lax.broadcasted_iota(jnp.int32, (n, n), 0)
    col = lax.broadcasted_iota(jnp.int32, (n, n), 1)
    work = jnp.concatenate([gram, jnp.where(row == col, 1.0, 0.0).astype(F32)], axis=1)
    below = lax.broadcasted_iota(jnp.int32, (n, 1), 0)
    for j in range(n):
        pivot = work[j:j + 1, :]
        scaled = pivot * lax.rsqrt(work[j:j + 1, j:j + 1])
        column = work[:, j:j + 1] * lax.rsqrt(work[j:j + 1, j:j + 1])
        work = jnp.where(below > j, work - column * scaled, jnp.where(below == j, scaled, work))
    return work[:, n:]


def exchange_kernel(groups, shards, sizes, act_ref, grad_ref, err_ref, q_ref,
                    all_ref, cols_ref, basis_ref, factor_ref,
                    a_send, e_high, e_low, e_buf, w_buf, l_buf, m_buf, z_send, z_buf, r_send, r_buf, s_send, s_buf, f_buf, x_buf,
                    sem_local, sem_e, sem_up, sem_down, sem_side, sem_block, *sems):
    zs, ys = sizes
    me, grp = lax.axis_index("shard"), lax.axis_index("grp")
    z, y = me // ys, me % ys
    tok, width = grad_ref.shape
    own = width // shards
    rank = q_ref.shape[0]
    part = rank // groups
    tiles = width // LANES
    step_rows = tok // CHUNKS

    barrier = pltpu.get_barrier_semaphore()
    for k in range(1, shards):
        pl.semaphore_signal(barrier, inc=1, device_id={"shard": (me + k) % shards}, device_id_type=pl.DeviceIdType.MESH)
    for k in range(1, groups):
        pl.semaphore_signal(barrier, inc=1, device_id={"grp": (grp + k) % groups}, device_id_type=pl.DeviceIdType.MESH)

    err_rows = e_buf.shape[1] // tiles
    loads = own // err_rows

    def err_copy(i, slot):
        return pltpu.make_async_copy(err_ref.at[pl.ds(i * err_rows * tiles, err_rows * tiles), :], e_buf.at[slot], sem_e.at[slot])

    err_copy(0, 0).start()

    for t in range(shards):
        a_send[t] = act_ref[:, t * own:(t + 1) * own]

    pl.semaphore_wait(barrier, shards - 1 + groups - 1)

    pending = []

    def send(axis, src, dst, send_sem, recv_sem, target):
        copy = pltpu.make_async_remote_copy(src_ref=src, dst_ref=dst, send_sem=send_sem, recv_sem=recv_sem,
                                            device_id={axis: target}, device_id_type=pl.DeviceIdType.MESH)
        return copy

    def spread(axis, count, index, src, buf, ssem, rsem):
        for k in range(1, count):
            target = (index + k) % count
            copy = send(axis, src(target), buf.at[index], ssem.at[k], rsem.at[k], target)
            copy.start()
            pending.append(copy)

    def collect(axis, count, index, buf, ssem, rsem):
        for k in range(1, count):
            slot = buf.at[(index + count - k) % count]
            send(axis, slot, slot, ssem.at[k], rsem.at[k], (index + k) % count).wait_recv()

    spread("shard", shards, me, lambda t: a_send.at[t], cols_ref, sems[0], sems[1])
    own_cols = pltpu.make_async_copy(a_send.at[me], cols_ref.at[me], sem_local.at[0])
    own_cols.start()

    def piece(c):
        return pl.ds(c * step_rows, step_rows)

    def block(owner, c):
        return all_ref.at[owner, piece(c), :]

    def up(owner, zsrc, c, src):
        return send("shard", src, block(owner, c), sem_up.at[zsrc, c], sem_block.at[owner, c], (z + 1) * ys + y)

    def down(owner, zsrc, c, src):
        return send("shard", src, block(owner, c), sem_down.at[zsrc, c], sem_block.at[owner, c], (z - 1) * ys + y)

    def side(owner, zsrc, c, src, k):
        return send("shard", src, block(owner, c), sem_side.at[k, zsrc, c], sem_block.at[owner, c], z * ys + (y + k) % ys)

    own_block = pltpu.make_async_copy(grad_ref, all_ref.at[me], sem_local.at[1])
    own_block.start()
    for c in range(CHUNKS):
        src = grad_ref.at[piece(c), :]

        @pl.when(z + 1 < zs)
        def _():
            up(me, z, c, src).start()

        @pl.when(z > 0)
        def _():
            down(me, z, c, src).start()

        for k in range(1, ys):
            side(me, z, c, src, k).start()

    def forward(step, c):
        @pl.when(z >= step)
        def _():
            zsrc = z - step
            owner = zsrc * ys + y
            up(owner, zsrc, c, block(owner, c)).wait_recv()

            @pl.when(z + 1 < zs)
            def _():
                up(owner, zsrc, c, block(owner, c)).start()

            for k in range(1, ys):
                side(owner, zsrc, c, block(owner, c), k).start()

        @pl.when(z + step < zs)
        def _():
            zsrc = z + step
            owner = zsrc * ys + y
            down(owner, zsrc, c, block(owner, c)).wait_recv()

            @pl.when(z > 0)
            def _():
                down(owner, zsrc, c, block(owner, c)).start()

            for k in range(1, ys):
                side(owner, zsrc, c, block(owner, c), k).start()

    events = [(step, c) for step in range(1, zs) for c in range(CHUNKS)]

    def advance(count):
        for _ in range(min(count, len(events))):
            forward(*events.pop(0))

    def load_step(i, slot):
        err_copy(i, slot).wait()

        @pl.when(i + 1 < loads)
        def _():
            err_copy(i + 1, 1 - slot).start()

        for t in range(tiles):
            high, low = split(e_buf[slot, pl.ds(t, err_rows, stride=tiles), :])
            rows = pl.ds(pl.multiple_of(i * err_rows, err_rows), err_rows)
            e_high[rows, t * LANES:(t + 1) * LANES] = high
            e_low[rows, t * LANES:(t + 1) * LANES] = low

    def load_body(i, carry):
        load_step(2 * i, 0)
        load_step(2 * i + 1, 1)
        return carry

    lax.fori_loop(0, loads // 2, load_body, 0)

    right = q_ref[...]
    for it in range(ITERS):
        sem = sems[2 + 14 * it:]
        w_buf[it, me] = dot2(right, grad_ref[...], NT)
        spread("shard", shards, me, lambda t: w_buf.at[it, me], w_buf.at[it], sem[0], sem[1])
        left = dot3(right, e_high[...], e_low[...], NT)
        if it == 0:
            own_cols.wait()
            collect("shard", shards, me, cols_ref, sems[0], sems[1])
        else:
            advance(1)
        collect("shard", shards, me, w_buf.at[it], sem[0], sem[1])
        for t in range(shards):
            left = left + dot2(w_buf[it, t], cols_ref[t], NN)
        l_buf[it, grp] = left
        spread("grp", groups, grp, lambda t: l_buf.at[it, grp], l_buf.at[it], sem[2], sem[3])
        advance(1)
        collect("grp", groups, grp, l_buf.at[it], sem[2], sem[3])
        left = l_buf[it, 0]
        for t in range(1, groups):
            left = left + l_buf[it, t]
        left = left * (1.0 / groups)
        m_buf[it, me] = lax.dot_general(left, left, NT, precision=lax.Precision.HIGHEST, preferred_element_type=F32)
        spread("shard", shards, me, lambda t: m_buf.at[it, me], m_buf.at[it], sem[4], sem[5])
        advance(1)
        collect("shard", shards, me, m_buf.at[it], sem[4], sem[5])
        gram = m_buf[it, 0]
        for t in range(1, shards):
            gram = gram + m_buf[it, t]
        basis = lax.dot_general(inverse_lower(gram), left, NN, precision=lax.Precision.HIGHEST, preferred_element_type=F32)
        for t in range(shards):
            z_send[it, t] = dot2(basis, cols_ref[t], NT)
        z_buf[it, me] = z_send[it, me]
        spread("shard", shards, me, lambda t: z_send.at[it, t], z_buf.at[it], sem[6], sem[7])
        advance(1)
        out = dot3(basis, e_high[...], e_low[...], NN)
        collect("shard", shards, me, z_buf.at[it], sem[6], sem[7])
        mine = z_buf[it, 0]
        for t in range(1, shards):
            mine = mine + z_buf[it, t]
        out = out + dot2(mine, grad_ref[...], NN)
        for t in range(groups):
            r_send[it, t] = out[t * part:(t + 1) * part, :]
        r_buf[it, grp] = r_send[it, grp]
        spread("grp", groups, grp, lambda t: r_send.at[it, t], r_buf.at[it], sem[8], sem[9])
        advance(1)
        collect("grp", groups, grp, r_buf.at[it], sem[8], sem[9])
        total = r_buf[it, 0]
        for t in range(1, groups):
            total = total + r_buf[it, t]
        for t in range(shards):
            s_send[it, t] = total[:, t * own:(t + 1) * own]
        s_buf[it, me] = s_send[it, me]
        spread("shard", shards, me, lambda t: s_send.at[it, t], s_buf.at[it], sem[10], sem[11])
        advance(1)
        collect("shard", shards, me, s_buf.at[it], sem[10], sem[11])
        total = s_buf[it, 0]
        for t in range(1, shards):
            total = total + s_buf[it, t]
        f_buf[it, me] = total * (1.0 / groups)
        spread("shard", shards, me, lambda t: f_buf.at[it, me], f_buf.at[it], sem[12], sem[13])
        collect("shard", shards, me, f_buf.at[it], sem[12], sem[13])
        for t in range(shards):
            x_buf[it, grp, :, t * own:(t + 1) * own] = f_buf[it, t]
        gsem = sems[2 + 14 * ITERS + 2 * it:]
        spread("grp", groups, grp, lambda t: x_buf.at[it, grp], x_buf.at[it], gsem[0], gsem[1])
        collect("grp", groups, grp, x_buf.at[it], gsem[0], gsem[1])
        right = jnp.concatenate([x_buf[it, t] for t in range(groups)], axis=0)
    basis_ref[...] = basis
    factor_ref[...] = right

    advance(len(events))
    own_block.wait()
    for k in range(1, ys):
        for zsrc in range(zs):
            for c in range(CHUNKS):
                owner = zsrc * ys + (y + k) % ys
                side(owner, zsrc, c, block(owner, c), k).wait_recv()
    for copy in pending:
        copy.wait_send()
    for c in range(CHUNKS):
        for zsrc in range(zs):
            owner = zsrc * ys + y
            src = block(owner, c)

            @pl.when((z + 1 < zs) & (zsrc <= z))
            def _():
                up(owner, zsrc, c, src).wait_send()

            @pl.when((z > 0) & (zsrc >= z))
            def _():
                down(owner, zsrc, c, src).wait_send()

            for k in range(1, ys):
                side(owner, zsrc, c, src, k).wait_send()


def finish_kernel(cols_ref, all_ref, err_ref, basis_ref, factor_ref, update_ref, next_ref, turned, turned_basis):
    own = turned.shape[0]
    count = err_ref.shape[0] // own

    @pl.when(pl.program_id(0) == 0)
    def _():
        turned[...] = cols_ref[...].T
        high, low = split(basis_ref[...].T)
        turned_basis[...] = jnp.concatenate([high, low, high], axis=1)

    high, low = split(factor_ref[...])
    update = lax.dot_general(turned_basis[...], jnp.concatenate([high, high, low], axis=0), NN, preferred_element_type=F32)
    gradient = lax.dot_general(turned[...], all_ref[...], NN, preferred_element_type=F32)
    rest = gradient - update
    for j in range(count):
        at = pl.ds(j, own, stride=count)
        lanes = slice(j * LANES, (j + 1) * LANES)
        update_ref[at, :] = update[:, lanes]
        next_ref[at, :] = err_ref[at, :] + rest[:, lanes]


def finish_block(cols_ref, all_ref, err_ref, basis_ref, factor_ref, update_ref, next_ref, turned, turned_basis):
    flat = lambda ref: ref.reshape(ref.shape[0] * ref.shape[1], LANES)
    finish_kernel(cols_ref, all_ref, flat(err_ref), basis_ref, factor_ref, flat(update_ref), flat(next_ref), turned, turned_basis)


def local(groups, shards, activations, out_grads, error, q_start):
    tok, width = activations.shape[1:]
    own = error.shape[1]
    rank = q_start.shape[1]
    tiles = width // LANES
    ys = 1
    while (2 * ys) ** 2 <= shards and shards % (2 * ys) == 0:
        ys *= 2
    zs = shards // ys
    part = rank // groups
    dma = pltpu.SemaphoreType.DMA
    stages = [shards] * 2
    for _ in range(ITERS):
        stages += [shards] * 2 + [groups] * 2 + [shards] * 4 + [groups] * 2 + [shards] * 4
    for _ in range(ITERS):
        stages += [groups] * 2
    vmem = pl.BlockSpec(memory_space=pltpu.VMEM)
    hbm = pl.BlockSpec(memory_space=pl.ANY)
    err_flat = error.reshape(own * tiles, LANES)
    gathered, cols, basis, factor = pl.pallas_call(
        functools.partial(exchange_kernel, groups, shards, (zs, ys)),
        out_shape=(
            jax.ShapeDtypeStruct((shards, tok, width), BF16),
            jax.ShapeDtypeStruct((shards, tok, own), BF16),
            jax.ShapeDtypeStruct((rank, own), F32),
            jax.ShapeDtypeStruct((rank, width), F32),
        ),
        in_specs=[vmem, vmem, hbm, vmem],
        out_specs=(hbm, vmem, vmem, vmem),
        scratch_shapes=[
            pltpu.VMEM((shards, tok, own), BF16),
            pltpu.VMEM((own, width), BF16),
            pltpu.VMEM((own, width), BF16),
            pltpu.VMEM((2, 32 * tiles, LANES), F32),
            pltpu.VMEM((ITERS, shards, rank, tok), F32),
            pltpu.VMEM((ITERS, groups, rank, own), F32),
            pltpu.VMEM((ITERS, shards, rank, rank), F32),
            pltpu.VMEM((ITERS, shards, rank, tok), F32),
            pltpu.VMEM((ITERS, shards, rank, tok), F32),
            pltpu.VMEM((ITERS, groups, part, width), F32),
            pltpu.VMEM((ITERS, groups, part, width), F32),
            pltpu.VMEM((ITERS, shards, part, own), F32),
            pltpu.VMEM((ITERS, shards, part, own), F32),
            pltpu.VMEM((ITERS, shards, part, own), F32),
            pltpu.VMEM((ITERS, groups, part, width), F32),
            dma((2,)),
            dma((2,)),
            dma((zs, CHUNKS)),
            dma((zs, CHUNKS)),
            dma((ys, zs, CHUNKS)),
            dma((shards, CHUNKS)),
        ] + [dma((count,)) for count in stages],
        compiler_params=pltpu.CompilerParams(collective_id=0, has_side_effects=True, vmem_limit_bytes=56 * 2 ** 20),
    )(activations[0], out_grads[0], err_flat, q_start[0])

    span = 8 if tiles % 8 == 0 else tiles
    tokens = shards * tok
    update, error_next = pl.pallas_call(
        finish_block,
        grid=(tiles // span,),
        out_shape=(jax.ShapeDtypeStruct((own, tiles, LANES), F32),) * 2,
        in_specs=[
            pl.BlockSpec((tokens, own), lambda i: (0, 0)),
            pl.BlockSpec((tokens, span * LANES), lambda i: (0, i)),
            pl.BlockSpec((own, span, LANES), lambda i: (0, i, 0)),
            pl.BlockSpec((rank, own), lambda i: (0, 0)),
            pl.BlockSpec((rank, span * LANES), lambda i: (0, i)),
        ],
        out_specs=(pl.BlockSpec((own, span, LANES), lambda i: (0, i, 0)),) * 2,
        scratch_shapes=[pltpu.VMEM((own, tokens), BF16), pltpu.VMEM((own, 3 * rank), BF16)],
        compiler_params=pltpu.CompilerParams(vmem_limit_bytes=56 * 2 ** 20),
    )(cols.reshape(tokens, own), gathered.reshape(tokens, width), error.reshape(own, tiles, LANES), basis, factor)
    return update.reshape(own, 1, width), error_next.reshape(1, own, 1, width), factor[None]


def solution(mesh):
    in_specs = (
        P(None, ("grp", "shard"), None),
        P(None, ("grp", "shard"), None),
        P("grp", "shard", None, None),
        P(),
    )
    out_specs = (P("shard", None, None), P("grp", "shard", None, None), P())
    body = functools.partial(local, mesh.shape["grp"], mesh.shape["shard"])
    return jax.shard_map(body, mesh=mesh, in_specs=in_specs, out_specs=out_specs, check_vma=False)
```
